32 devices in a mesh: groups: 2 (over y), cuts: 4 (over z), mesh: 2 (over x), sub: 2 (over core).
Axes of the slice: x: 2, y: 2, z: 4, core: 2. Of those that a mesh axis runs over, the one named last changes fastest.
Arguments:
- couplings: float32 [64, 64, 256], P(('mesh', 'sub')), may hold values from 0 to 0.004464286
- edge_mask: int32 [64, 3], P(('mesh', 'sub')), may hold values 0 or 1
- slice_mass: float32 [8, 4096], P(('groups', 'cuts'), ('mesh', 'sub')), parts along dimension 0, may hold values from 0.003 to 700
- sources: float32 [8, 2, 4096], P(('groups', 'cuts'), None, ('mesh', 'sub')), parts along dimension 0, may hold values from -20 to 20
- slice_states: float32 [8, 4096], P(('groups', 'cuts'), ('mesh', 'sub')), parts along dimension 0, may hold values from -6 to 6
Outputs:
- new_states: float32 [8, 4096], P(('groups', 'cuts'), ('mesh', 'sub')), parts along dimension 0
- defect: float32 [8, 4096], P(('groups', 'cuts'), ('mesh', 'sub')), parts along dimension 0
The draws below stay inside these ranges and needn't reach their ends.
There are 2 independent parts, one for each index of `groups`. The reference program is written for one: setup_inputs(seed, part) draws one part's arguments, and reference() takes and returns one part's arrays. A program takes and returns all parts, laid end to end along the dimension named above; an argument that names none is the same for every part. Nothing has to cross between parts.
All inputs are finite; a program needn't handle non-finite values. No bound on the sum of `edge_mask` on one device may be relied on, other than what follows from the above.
Results may differ from the reference program's by a relative error of at most 0.0003.
Values sent between devices are 32-bit elements; how exact they have to be, the bound alone decides.
A program may use at most 64 MiB of HBM per device.

```python
import math
import jax
import jax.numpy as jnp
from jax import lax

BLOCK = 64
REACH = 3
CG_ITERS = 4
STEPS = 2
SWEEPS = 2
PERIOD_SLICES = 4
NBLK = 64
UNKNOWN_TOTAL = 4096


def draw_slice_mass(key, part):
    key = jax.random.fold_in(key, 11)
    random_keys = jax.random.split(key, 4)
    lowest = 0.5
    base_mass = jnp.exp(jax.random.uniform(random_keys[0], (1, UNKNOWN_TOTAL), jnp.float32, math.log(lowest), math.log(500.0)))
    varied = jnp.exp(jax.random.uniform(random_keys[1], (PERIOD_SLICES, UNKNOWN_TOTAL), jnp.float32, math.log(0.7), math.log(1.4)))
    pulse_slice = (jax.random.randint(random_keys[2], (PERIOD_SLICES, 1), 0, 5) == 0).astype(jnp.float32)
    pulse_size = jax.random.uniform(random_keys[3], (PERIOD_SLICES, UNKNOWN_TOTAL), jnp.float32, 0.01, 0.04)
    multiplier = 1.0 + pulse_slice * (pulse_size - 1.0)
    return base_mass * varied * multiplier


def draw_sources(key, part):
    key = jax.random.fold_in(key, 23)
    random_keys = jax.random.split(key, 2)
    full_shape = (PERIOD_SLICES, STEPS, UNKNOWN_TOTAL)
    position = jnp.arange(UNKNOWN_TOTAL, dtype=jnp.float32) / UNKNOWN_TOTAL
    ramp = 0.5 + position
    block_scale = jnp.exp(jax.random.uniform(random_keys[0], (PERIOD_SLICES, STEPS, NBLK, 1), jnp.float32, 0.0, math.log(10.0)))
    block_scale = jnp.broadcast_to(block_scale, (PERIOD_SLICES, STEPS, NBLK, BLOCK)).reshape(full_shape)
    rough = jnp.clip(jax.random.normal(random_keys[1], full_shape, jnp.float32), -4.0, 4.0)
    return 0.3 * ramp * block_scale * rough


def with_ends(result, own_key, low, top_value):
    place = [jax.random.randint(jax.random.fold_in(own_key, axis), (), 0, length) for axis, length in enumerate(result.shape)]
    widest = result.shape.index(max(result.shape))
    beside = place[:widest] + [(place[widest] + 1) % result.shape[widest]] + place[widest + 1:]
    return result.at[tuple(place)].set(low).at[tuple(beside)].set(top_value)


def steps_of(own_key, dims, cuts, low, high):
    def one(axis_at, parts):
        draws = jax.random.uniform(jax.random.fold_in(jax.random.fold_in(own_key, 6), axis_at), (parts,), jnp.float32, low / len(cuts), high / len(cuts))
        return jnp.repeat(jnp.exp(draws), dims[axis_at] // parts).reshape((-1,) + (1,) * (len(dims) - axis_at - 1))

    level = one(*cuts[0])
    for cut in cuts[1:]:
        level = level * one(*cut)
    return level


def gaussian(stream_key, extent, width, reach, shards=(), kind=jnp.bfloat16):
    loudness = steps_of(stream_key, extent, shards, -0.22, 0.18) if shards else 1.0
    entries = jax.random.normal(stream_key, extent, jnp.float32) * width * loudness
    return jnp.minimum(jnp.maximum(entries, -reach), reach).astype(kind)


def setup_inputs(seed: int = 0, part: int = 0) -> dict:
    key_list = jax.random.split(jax.random.key(seed), 6)
    part_splits = jax.random.split(jax.random.fold_in(key_list[5], part), 6)
    couplings = jnp.clip(0.004464286 * jax.random.uniform(key_list[0], (NBLK, BLOCK, (REACH + 1) * BLOCK), jnp.float32) ** steps_of(key_list[0], (NBLK, BLOCK, (REACH + 1) * BLOCK), ((0, 4),), -0.2, 0.2), 0.0, 0.004464286)
    edge_mask = with_ends((jax.random.randint(key_list[1], (NBLK, REACH), 0, 4) < 3).astype(jnp.int32), jax.random.fold_in(key_list[1], 1), 0, 1)
    slice_mass = draw_slice_mass(jax.random.fold_in(jax.random.fold_in(key_list[5], part), 71), part)
    sources = draw_sources(jax.random.fold_in(jax.random.fold_in(key_list[5], part), 71), part)
    slice_states = gaussian(part_splits[4], (PERIOD_SLICES, UNKNOWN_TOTAL), 1.0, 6.0, ((0, 4), (1, 4)), jnp.float32)
    return {"couplings": couplings, "edge_mask": edge_mask, "slice_mass": slice_mass, "sources": sources, "slice_states": slice_states}


HIGHEST = lax.Precision.HIGHEST


def couple(couplings, edge_mask, vectors):
    block_size = couplings.shape[1]
    diag_blocks = couplings[:, :, :block_size]
    off_blocks = couplings[:, :, block_size:]
    unit_matrix = jnp.eye(block_size, dtype=jnp.float32)
    own_blocks = 0.5 * (diag_blocks + jnp.swapaxes(diag_blocks, 1, 2)) * (1.0 - unit_matrix)
    mask_float = edge_mask.astype(jnp.float32)
    window = jnp.concatenate(
        [jnp.roll(vectors, -offset, axis=1) * mask_float[None, :, offset - 1:offset] for offset in range(1, REACH + 1)],
        axis=2)
    summed = jnp.einsum("bij,sbj->sbi", own_blocks, vectors, precision=HIGHEST)
    summed = summed + jnp.einsum("bij,sbj->sbi", off_blocks, window, precision=HIGHEST)
    for offset in range(1, REACH + 1):
        segment = off_blocks[:, :, (offset - 1) * block_size:offset * block_size]
        masked = vectors * mask_float[None, :, offset - 1:offset]
        pushed = jnp.einsum("bji,sbj->sbi", segment, masked, precision=HIGHEST)
        summed = summed + jnp.roll(pushed, offset, axis=1)
    return summed


def chain_step(carry, paired):
    return (paired[0] * carry[0], paired[0] * carry[1] + paired[1]), carry


def reference(couplings, edge_mask, slice_mass, sources, slice_states):
    block_size = couplings.shape[1]
    blocks_all = couplings.shape[0]
    slices = slice_mass.shape[0]
    summed_rows = couple(couplings, edge_mask, jnp.ones((1, blocks_all, block_size), jnp.float32)).reshape(-1)
    diagonal = slice_mass + summed_rows[None, :]

    def operate(vectors):
        coupled = couple(couplings, edge_mask, vectors.reshape(slices, blocks_all, block_size))
        return diagonal * vectors - coupled.reshape(slices, -1)

    def total_of(values):
        return jnp.sum(values, axis=1, keepdims=True)

    def solve(rhs):
        solution = jnp.zeros_like(rhs)
        residual = rhs
        direction = rhs
        norm_now = total_of(residual * residual)
        for iteration in range(CG_ITERS):
            applied = operate(direction)
            step_length = norm_now / total_of(direction * applied)
            solution = solution + step_length * direction
            if iteration + 1 < CG_ITERS:
                residual = residual - step_length * applied
                norm_next = total_of(residual * residual)
                direction = residual + (norm_next / norm_now) * direction
                norm_now = norm_next
        return solution

    def propagate(states):
        current = states
        for section in range(STEPS):
            current = solve(slice_mass * current + sources[:, section, :])
        return current

    rate = slice_mass / (slice_mass + STEPS * summed_rows[None, :])
    states = slice_states
    defect = jnp.zeros_like(states)
    for sweep_index in range(SWEEPS):
        fine_end = propagate(states)
        offset_term = fine_end - rate * states
        start_map = (jnp.ones_like(rate[0]), jnp.zeros_like(rate[0]))
        (loop_rate, loop_offset), (rates_before, offsets_before) = lax.scan(chain_step, start_map, (rate, offset_term))
        first_state = loop_offset / (1.0 - loop_rate)
        new_states = rates_before * first_state[None, :] + offsets_before
        if sweep_index == SWEEPS - 1:
            defect = jnp.roll(fine_end, 1, axis=0) - states
        states = new_states
    return states, defect
```

```python
import functools

import jax
import jax.numpy as jnp
from jax import lax
from jax.experimental import pallas as pl
from jax.experimental.pallas import tpu as pltpu
from jax.sharding import PartitionSpec as P

REACH = 3
CG_ITERS = 4
SWEEPS = 2
BLOCK = 64
LANES = 128
ROWS = 8
HALO = 2 * LANES
MESH = pl.DeviceIdType.MESH


def kernel(sizes, coup, mask, mass_ref, src_ref, st_ref, new_ref, def_ref,
           W, hsend, hrecv, vsend, vrecv, send, recv, csend, crecv, spread,
           hsem, vsem, xs_sem, xr_sem, cs_sem, cr_sem):
    n_mesh, n_sub, n_cut = sizes
    n_sec = n_mesh * n_sub
    blocks = coup.shape[0]
    groups = blocks // 2
    local = blocks * BLOCK
    wide = local + 2 * HALO
    tiles = wide // LANES
    steps = src_ref.shape[1]

    sector = lax.axis_index("mesh") * n_sub + lax.axis_index("sub")
    cut = lax.axis_index("cuts")

    def sector_id(distance):
        other = lax.rem(sector + distance, n_sec)
        return {"mesh": other // n_sub, "sub": lax.rem(other, n_sub)}

    def cut_id(distance):
        return {"cuts": lax.rem(cut + distance, n_cut)}

    barrier = pltpu.get_barrier_semaphore()
    for d in range(1, n_sec):
        pl.semaphore_signal(barrier, inc=1, device_id=sector_id(d), device_id_type=MESH)
    for d in range(1, n_cut):
        pl.semaphore_signal(barrier, inc=1, device_id=cut_id(d), device_id_type=MESH)

    low_half = lax.broadcasted_iota(jnp.int32, (BLOCK, LANES), 1) < BLOCK
    low_row = lax.broadcasted_iota(jnp.int32, (ROWS, LANES), 1) < BLOCK
    row = lax.broadcasted_iota(jnp.int32, (ROWS, LANES), 0)

    def factors(b):
        return [mask[b, k].astype(jnp.float32) for k in range(REACH)]

    def masked(b):
        m = factors(b)
        near = coup[b, :, :LANES] * jnp.where(low_half, 1.0, m[0])
        far = coup[b, :, LANES:] * jnp.where(low_half, m[1], m[2])
        return near, far

    def turned(x):
        return pltpu.roll(x, BLOCK, 1)

    near1, far1 = masked(blocks - 1)
    _, far2 = masked(blocks - 2)
    _, far3 = masked(blocks - 3)
    near1t, far1t, far3t = turned(near1), turned(far1), turned(far3)
    hsend[0] = jnp.where(low_half, near1t, far1t)
    hsend[1] = far2
    hsend[2] = jnp.where(low_half, far3t, far1)
    for i, at in enumerate((local - HALO, 0)):
        vsend[i, 0:1, :] = mass_ref[0:1, at:at + HALO]
        vsend[i, 1:2, :] = st_ref[0:1, at:at + HALO]
        for s in range(steps):
            vsend[i, 2 + s:3 + s, :] = src_ref[0, s:s + 1, at:at + HALO]

    pl.semaphore_wait(barrier, n_sec - 1 + n_cut - 1)

    right, left = sector_id(1), sector_id(n_sec - 1)
    first = [
        pltpu.make_async_remote_copy(hsend, hrecv, hsem.at[0], hsem.at[1], device_id=right, device_id_type=MESH),
        pltpu.make_async_remote_copy(vsend.at[0], vrecv.at[0], vsem.at[0], vsem.at[1], device_id=right, device_id_type=MESH),
        pltpu.make_async_remote_copy(vsend.at[1], vrecv.at[1], vsem.at[2], vsem.at[3], device_id=left, device_id_type=MESH),
    ]
    for copy in first:
        copy.start()

    def put(g, at, block):
        high = block.astype(jnp.bfloat16)
        low = (block - high.astype(jnp.float32)).astype(jnp.bfloat16)
        W[g, at * BLOCK:(at + 1) * BLOCK, :LANES] = high
        W[g, at * BLOCK:(at + 1) * BLOCK, LANES:] = low

    unit = lax.broadcasted_iota(jnp.int32, (BLOCK, LANES), 0) == lax.rem(
        lax.broadcasted_iota(jnp.int32, (BLOCK, LANES), 1), BLOCK)
    zero = jnp.zeros((BLOCK, LANES), jnp.float32)
    for g in range(groups):
        n0, f0 = masked(2 * g)
        n1, f1 = masked(2 * g + 1)
        near_t = jnp.concatenate([n0, n1], axis=0).T
        far_t = jnp.concatenate([f0, f1], axis=0).T
        own_t, k1_t = near_t[:BLOCK], near_t[BLOCK:]
        k2_t, k3_t = far_t[:BLOCK], far_t[BLOCK:]
        n1t, f1t = turned(n1), turned(f1)
        put(g, 4, jnp.where(low_half, jnp.where(unit, 0.0, 0.5 * (n0 + own_t)), n0))
        put(g, 5, jnp.where(low_half, k1_t, jnp.where(unit, 0.0, 0.5 * (n1t + own_t))))
        put(g, 6, jnp.where(low_half, k2_t, k1_t))
        put(g, 7, jnp.where(low_half, k3_t, k2_t))
        put(g, 0, jnp.where(low_half, zero, k3_t))
        if g + 1 < groups:
            put(g + 1, 2, f0)
            put(g + 1, 3, jnp.where(low_half, n1t, f1t))
        if g + 2 < groups:
            put(g + 2, 1, jnp.where(low_half, f1t, zero))

    for copy in first:
        copy.wait()
    put(0, 3, hrecv[0])
    put(0, 2, hrecv[1])
    z = hrecv[2]
    put(0, 1, jnp.where(low_half, z, zero))
    put(1, 1, jnp.where(low_half, turned(z), zero))

    def spanned(at, middle):
        whole = jnp.concatenate([vrecv[0, at:at + 1, :], middle, vrecv[1, at:at + 1, :]], axis=1)
        return jnp.broadcast_to(whole, (ROWS, wide))

    def total(x):
        x = x + pltpu.roll(x, 4, 0)
        x = x + pltpu.roll(x, 2, 0)
        return x + pltpu.roll(x, 1, 0)

    row_wide = lax.broadcasted_iota(jnp.int32, (ROWS, wide), 0)

    def coupled(v):
        h = v.astype(jnp.bfloat16).astype(jnp.float32)
        rest = v - h
        m = rest.astype(jnp.bfloat16).astype(jnp.float32)
        parts = jnp.where(row_wide == 0, h, jnp.where(row_wide == 1, m, jnp.where(row_wide == 2, rest - m, 0.0)))
        cast = parts.astype(jnp.bfloat16)
        out = []
        for g in range(groups):
            at = g * LANES
            ends = jnp.where(low_row, parts[:, at + 4 * LANES:at + 5 * LANES], parts[:, at:at + LANES])
            lhs = jnp.concatenate([ends.astype(jnp.bfloat16), cast[:, at + LANES:at + 4 * LANES]], axis=1)
            r = jnp.dot(lhs, W[g], preferred_element_type=jnp.float32)
            out.append(total(r[:, :LANES] + r[:, LANES:]))
        return jnp.concatenate(out, axis=1)

    def stacked(*values):
        message = values[-1]
        for i in range(len(values) - 2, -1, -1):
            message = jnp.where(row == i, values[i], message)
        return message

    def folded(x):
        parts = [x[:, i * LANES:(i + 1) * LANES] for i in range(groups)]
        while len(parts) > 1:
            parts = [sum(parts[i:i + 2]) for i in range(0, len(parts), 2)]
        return parts[0]

    def exchange(slot, w, rr, rw, sums):
        end = local - HALO
        send[slot, 0] = stacked(w[:, end:end + LANES], w[:, end + LANES:], rr, rw,
                                sums[:, end:end + LANES], sums[:, end + LANES:])
        send[slot, 1] = stacked(w[:, :LANES], w[:, LANES:HALO], rr, rw,
                                sums[:, :LANES], sums[:, LANES:HALO])
        copies = []
        for d in range(1, n_sec):
            copies.append(pltpu.make_async_remote_copy(
                send.at[slot, 1 if d == n_sec - 1 else 0], recv.at[slot, d - 1],
                xs_sem.at[slot, d - 1], xr_sem.at[slot, d - 1],
                device_id=sector_id(d), device_id_type=MESH))
        for copy in copies:
            copy.start()
        for copy in copies:
            copy.wait()

        def line(d, i):
            return jnp.broadcast_to(recv[slot, d - 1, i:i + 1, :], (ROWS, LANES))

        for d in range(1, n_sec):
            rr = rr + line(d, 2)
            rw = rw + line(d, 3)
        w = jnp.concatenate([line(1, 0), line(1, 1), w, line(n_sec - 1, 0), line(n_sec - 1, 1)], axis=1)
        return w, jnp.sum(rr, axis=1, keepdims=True), jnp.sum(rw, axis=1, keepdims=True)

    mass = spanned(0, mass_ref[...])
    states = spanned(1, st_ref[...])
    sums = coupled(jnp.ones((ROWS, wide), jnp.float32))
    diagonal = mass[:, HALO:HALO + local] + sums

    def solve(rhs):
        r = rhs
        x = p = s = alpha = old = None
        for it in range(CG_ITERS):
            mine = r[:, HALO:HALO + local]
            w = diagonal * mine - coupled(r)
            w, rr, rw = exchange(it % 2, w, folded(mine * mine), folded(mine * w), sums)
            if it == 0:
                alpha = rr / rw
                p, s = r, w
                x = alpha * p
            else:
                beta = rr / old
                alpha = rr / (rw - beta * rr / alpha)
                p, s = r + beta * p, w + beta * s
                x = x + alpha * p
            if it + 1 < CG_ITERS:
                r = r - alpha * s
            old = rr
        return x

    def to_rows(ref, x):
        for t in range(tiles):
            ref[t:t + 1, :] = x[0:1, t * LANES:(t + 1) * LANES]

    rate = None
    for sweep in range(SWEEPS):
        def section(i, current):
            source = jnp.concatenate(
                [vrecv[0, pl.ds(2 + i, 1), :], src_ref[0, pl.ds(i, 1), :], vrecv[1, pl.ds(2 + i, 1), :]], axis=1)
            return solve(mass * current + jnp.broadcast_to(source, (ROWS, wide)))

        fine = lax.fori_loop(0, steps, section, states)
        if sweep == 0:
            slot = CG_ITERS - 1 - (CG_ITERS - 1) // 2 * 2
            edge = [jnp.broadcast_to(recv[slot, d, i:i + 1, :], (ROWS, LANES))
                    for d in (0, n_sec - 2) for i in (4, 5)]
            all_sums = jnp.concatenate([edge[0], edge[1], sums, edge[2], edge[3]], axis=1)
            rate = mass / (mass + steps * all_sums)
        offset = fine - rate * states
        to_rows(csend.at[sweep, 0], offset)
        to_rows(csend.at[sweep, 1], rate if sweep == 0 else fine)
        copies = [pltpu.make_async_remote_copy(
            csend.at[sweep], crecv.at[sweep, cut], cs_sem.at[sweep, d - 1], cr_sem.at[sweep, d - 1],
            device_id=cut_id(d), device_id_type=MESH) for d in range(1, n_cut)]
        for copy in copies:
            copy.start()
        crecv[sweep, cut] = csend[sweep]
        for copy in copies:
            copy.wait()
        p_run = jnp.ones((tiles, LANES), jnp.float32)
        q_run = jnp.zeros((tiles, LANES), jnp.float32)
        p_mine, q_mine = p_run, q_run
        for j in range(n_cut):
            here = cut == j
            p_mine = jnp.where(here, p_run, p_mine)
            q_mine = jnp.where(here, q_run, q_mine)
            a = crecv[0, j, 1, :tiles]
            b = crecv[sweep, j, 0, :tiles]
            p_run, q_run = a * p_run, a * q_run + b
        new = p_mine * (q_run / (1.0 - p_run)) + q_mine
        if sweep == SWEEPS - 1:
            arrived = crecv[sweep, lax.rem(cut + n_cut - 1, n_cut), 1, :tiles]
            spread[:tiles, :] = arrived
            for t in range(2, tiles - 2):
                at = (t - 2) * LANES
                def_ref[0:1, at:at + LANES] = spread[t:t + 1, :] - states[0:1, t * LANES:(t + 1) * LANES]
                new_ref[0:1, at:at + LANES] = new[t:t + 1, :]
        else:
            spread[:tiles, :] = new
            states = jnp.concatenate(
                [jnp.broadcast_to(spread[t:t + 1, :], (ROWS, LANES)) for t in range(tiles)], axis=1)


def shards(sizes, couplings, edge_mask, slice_mass, sources, slice_states):
    n_mesh, n_sub, n_cut = sizes
    n_sec = n_mesh * n_sub
    blocks = couplings.shape[0]
    wide = blocks * BLOCK + 2 * HALO
    tiles = wide // LANES
    lines = -(-tiles // ROWS) * ROWS
    steps = sources.shape[1]
    vrows = -(-(2 + steps) // ROWS) * ROWS
    f32 = jnp.float32
    vmem = pl.BlockSpec(memory_space=pltpu.VMEM)
    out = jax.ShapeDtypeStruct(slice_states.shape, f32)
    return pl.pallas_call(
        functools.partial(kernel, sizes),
        out_shape=(out, out),
        in_specs=[vmem, pl.BlockSpec(memory_space=pltpu.SMEM), vmem, vmem, vmem],
        out_specs=(vmem, vmem),
        scratch_shapes=[
            pltpu.VMEM((blocks // 2, 8 * BLOCK, 2 * LANES), jnp.bfloat16),
            pltpu.VMEM((3, BLOCK, LANES), f32),
            pltpu.VMEM((3, BLOCK, LANES), f32),
            pltpu.VMEM((2, vrows, HALO), f32),
            pltpu.VMEM((2, vrows, HALO), f32),
            pltpu.VMEM((2, 2, ROWS, LANES), f32),
            pltpu.VMEM((2, n_sec - 1, ROWS, LANES), f32),
            pltpu.VMEM((SWEEPS, 2, lines, LANES), f32),
            pltpu.VMEM((SWEEPS, n_cut, 2, lines, LANES), f32),
            pltpu.VMEM((lines, LANES), f32),
            pltpu.SemaphoreType.DMA((2,)),
            pltpu.SemaphoreType.DMA((4,)),
            pltpu.SemaphoreType.DMA((2, n_sec - 1)),
            pltpu.SemaphoreType.DMA((2, n_sec - 1)),
            pltpu.SemaphoreType.DMA((SWEEPS, n_cut - 1)),
            pltpu.SemaphoreType.DMA((SWEEPS, n_cut - 1)),
        ],
        compiler_params=pltpu.CompilerParams(
            collective_id=0, has_side_effects=True, vmem_limit_bytes=32 * 1024 * 1024),
    )(couplings, edge_mask, slice_mass, sources, slice_states)


def solution(mesh):
    rows = P(("groups", "cuts"), ("mesh", "sub"))
    placed = (
        P(("mesh", "sub"), None, None),
        P(("mesh", "sub"), None),
        rows,
        P(("groups", "cuts"), None, ("mesh", "sub")),
        rows,
    )
    sizes = (mesh.shape["mesh"], mesh.shape["sub"], mesh.shape["cuts"])
    return jax.shard_map(
        functools.partial(shards, sizes),
        mesh=mesh,
        in_specs=placed,
        out_specs=(rows, rows),
        check_vma=False,
    )
```

```python
import functools

import jax
import jax.numpy as jnp
from jax import lax
from jax.experimental import pallas as pl
from jax.experimental.pallas import tpu as pltpu
from jax.sharding import PartitionSpec as P

REACH = 3
CG_ITERS = 4
SWEEPS = 2
BLOCK = 64
LANES = 128
ROWS = 8
HALO = 3 * LANES
BEFORE = 2 * REACH
MESH = pl.DeviceIdType.MESH


def kernel(sizes, coup, mask, mass_ref, src_ref, st_ref, new_ref, def_ref,
           W, ext, fac, vsend, vrecv, tsend, trecv, send, recv, csend, crecv, spread,
           lsem, hsem, fsem, vsem, ts_sem, tr_sem, xs_sem, xr_sem, cs_sem, cr_sem):
    n_mesh, n_sub, n_cut = sizes
    n_sec = n_mesh * n_sub
    blocks = coup.shape[0]
    groups = blocks // 2
    local = blocks * BLOCK
    wide = local + 2 * HALO
    tiles = wide // LANES
    edge = HALO // LANES
    steps = src_ref.shape[1]

    sector = lax.axis_index("mesh") * n_sub + lax.axis_index("sub")
    cut = lax.axis_index("cuts")

    def sector_id(distance):
        other = lax.rem(sector + distance, n_sec)
        return {"mesh": other // n_sub, "sub": lax.rem(other, n_sub)}

    def cut_id(distance):
        return {"cuts": lax.rem(cut + distance, n_cut)}

    barrier = pltpu.get_barrier_semaphore()
    for d in range(1, n_sec):
        pl.semaphore_signal(barrier, inc=1, device_id=sector_id(d), device_id_type=MESH)
    for d in range(1, n_cut):
        pl.semaphore_signal(barrier, inc=1, device_id=cut_id(d), device_id_type=MESH)
    fetch = pltpu.make_async_copy(coup, ext.at[BEFORE:BEFORE + blocks], lsem)
    fetch.start()

    low_half = lax.broadcasted_iota(jnp.int32, (BLOCK, LANES), 1) < BLOCK
    low_row = lax.broadcasted_iota(jnp.int32, (ROWS, LANES), 1) < BLOCK
    low_line = lax.broadcasted_iota(jnp.int32, (1, LANES), 1) < BLOCK
    row = lax.broadcasted_iota(jnp.int32, (ROWS, LANES), 0)
    zero = jnp.zeros((BLOCK, LANES), jnp.float32)

    for b in range(blocks):
        m = [mask[k, b].astype(jnp.float32) for k in range(REACH)]
        fac[BEFORE + b, 0:1, :] = jnp.where(low_line, 1.0, m[0])
        fac[BEFORE + b, 1:2, :] = jnp.where(low_line, m[1], m[2])
    last = BEFORE + blocks + REACH
    fac[last] = jnp.zeros((2, LANES), jnp.float32)
    ext[last, :, :LANES] = zero
    ext[last, :, LANES:] = zero
    for b in range(2):
        ext[b, :, :LANES] = zero
    for i, at in enumerate((local - HALO, 0)):
        vsend[i, 0:1, :] = mass_ref[0:1, at:at + HALO]
        vsend[i, 1:2, :] = st_ref[0:1, at:at + HALO]
        for s in range(steps):
            vsend[i, 2 + s:3 + s, :] = src_ref[0, s:s + 1, at:at + HALO]

    def folded(x):
        parts = [x[:, i * LANES:(i + 1) * LANES] for i in range(x.shape[1] // LANES)]
        while len(parts) > 1:
            parts = [sum(parts[i:i + 2]) for i in range(0, len(parts), 2)]
        return parts[0]

    tsend[...] = jnp.broadcast_to(folded(mass_ref[...]), (ROWS, LANES))

    pl.semaphore_wait(barrier, n_sec - 1 + n_cut - 1)

    right, left = sector_id(1), sector_id(n_sec - 1)
    after = BEFORE + blocks

    def to(src, dst, sems, i, who):
        return pltpu.make_async_remote_copy(
            src, dst, sems.at[i], sems.at[i + 1], device_id=who, device_id_type=MESH)

    first = [
        to(coup.at[blocks - 4:blocks], ext.at[2:BEFORE], hsem, 0, right),
        to(coup.at[0:REACH], ext.at[after:last], hsem, 2, left),
        to(coup.at[blocks - BEFORE:blocks - 4, :, LANES:], ext.at[0:2, :, LANES:], hsem, 4, right),
        to(fac.at[blocks:after], fac.at[0:BEFORE], fsem, 0, right),
        to(fac.at[BEFORE:BEFORE + REACH], fac.at[after:last], fsem, 2, left),
        to(vsend.at[0], vrecv.at[0], vsem, 0, right),
        to(vsend.at[1], vrecv.at[1], vsem, 2, left),
    ]
    for d in range(1, n_sec):
        first.append(pltpu.make_async_remote_copy(
            tsend, trecv.at[d - 1], ts_sem.at[d - 1], tr_sem.at[d - 1],
            device_id=sector_id(d), device_id_type=MESH))
    for copy in first[3:] + first[:3]:
        copy.start()

    def turned(x):
        return pltpu.roll(x, BLOCK, 1)

    n_w = groups + 4

    def put(g, at, block):
        if not 0 <= g < n_w:
            return
        high = block.astype(jnp.bfloat16)
        low = (block - high.astype(jnp.float32)).astype(jnp.bfloat16)
        W[g, at * BLOCK:(at + 1) * BLOCK, :LANES] = high
        W[g, at * BLOCK:(at + 1) * BLOCK, LANES:] = low

    unit = lax.broadcasted_iota(jnp.int32, (BLOCK, LANES), 0) == lax.rem(
        lax.broadcasted_iota(jnp.int32, (BLOCK, LANES), 1), BLOCK)

    def masked(b):
        return ext[b, :, :LANES] * fac[b, 0:1, :], ext[b, :, LANES:] * fac[b, 1:2, :]

    def build(pair):
        g = pair + 2
        n0, f0 = masked(2 * pair + BEFORE)
        n1, f1 = masked(2 * pair + BEFORE + 1)
        n1t, f1t = turned(n1), turned(f1)
        put(g + 1, 2, f0)
        put(g + 1, 3, jnp.where(low_half, n1t, f1t))
        put(g + 2, 1, jnp.where(low_half, f1t, zero))
        if g < 0:
            return
        near_t = jnp.concatenate([n0, n1], axis=0).T
        far_t = jnp.concatenate([f0, f1], axis=0).T
        own_t, k1_t = near_t[:BLOCK], near_t[BLOCK:]
        k2_t, k3_t = far_t[:BLOCK], far_t[BLOCK:]
        put(g, 4, jnp.where(low_half, jnp.where(unit, 0.0, 0.5 * (n0 + own_t)), n0))
        put(g, 5, jnp.where(low_half, k1_t, jnp.where(unit, 0.0, 0.5 * (n1t + own_t))))
        put(g, 6, jnp.where(low_half, k2_t, k1_t))
        put(g, 7, jnp.where(low_half, k3_t, k2_t))
        put(g, 0, jnp.where(low_half, zero, k3_t))

    put(0, 1, zero)
    fetch.wait()
    for pair in range(groups):
        build(pair)
    for copy in first:
        copy.wait()
    for pair in (-3, -2, -1, groups, groups + 1):
        build(pair)

    def spanned(at, middle):
        whole = jnp.concatenate([vrecv[0, at:at + 1, :], middle, vrecv[1, at:at + 1, :]], axis=1)
        return jnp.broadcast_to(whole, (ROWS, wide))

    def total(x):
        x = x + pltpu.roll(x, 4, 0)
        x = x + pltpu.roll(x, 2, 0)
        return x + pltpu.roll(x, 1, 0)

    def tile(x, i):
        return x[:, i * LANES:(i + 1) * LANES]

    def coupled(vectors, begin, count):
        width = vectors[0].shape[1]
        rows = lax.broadcasted_iota(jnp.int32, (ROWS, width), 0)
        parts = jnp.zeros((ROWS, width), jnp.float32)
        for i, v in enumerate(vectors):
            h = v.astype(jnp.bfloat16).astype(jnp.float32)
            rest = v - h
            m = rest.astype(jnp.bfloat16).astype(jnp.float32)
            for j, part in enumerate((h, m, rest - m)):
                parts = jnp.where(rows == 3 * i + j, part, parts)
        cast = parts.astype(jnp.bfloat16)
        blank = jnp.zeros((ROWS, LANES), jnp.float32)
        n_tiles = width // LANES
        out = [[] for _ in vectors]
        for t in range(count):
            centre = t + begin
            up = tile(parts, centre + 2) if centre + 2 < n_tiles else blank
            down = tile(parts, centre - 2) if centre >= 2 else blank
            ends = jnp.where(low_row, up, down).astype(jnp.bfloat16)
            lhs = jnp.concatenate([ends, cast[:, (centre - 1) * LANES:(centre + 2) * LANES]], axis=1)
            g = t + (n_w - count) // 2
            r = jnp.dot(lhs, W[g], preferred_element_type=jnp.float32)
            r = r[:, :LANES] + r[:, LANES:]
            if len(vectors) == 1:
                out[0].append(total(r))
            else:
                out[0].append(total(jnp.where(row < 3, r, 0.0)))
                out[1].append(total(jnp.where(row < 3, 0.0, r)))
        return [jnp.concatenate(o, axis=1) for o in out]

    def stacked(values):
        halves = []
        for at in (0, ROWS):
            message = jnp.zeros((ROWS, LANES), jnp.float32)
            for i in range(ROWS):
                if at + i in values:
                    message = jnp.where(row == i, values[at + i], message)
            halves.append(message)
        return jnp.concatenate(halves, axis=0)

    def exchange(slot, dots, rims):
        ends = []
        for side in range(2):
            values = dict(enumerate(dots))
            for at, v in rims:
                for i in range(edge):
                    values[at + i] = tile(v, i if side else groups - edge + i)
            ends.append(stacked(values))
            send[slot, side] = ends[side]
        copies = []
        for d in range(1, n_sec):
            copies.append(pltpu.make_async_remote_copy(
                send.at[slot, 1 if d == n_sec - 1 else 0], recv.at[slot, d - 1],
                xs_sem.at[slot, d - 1], xr_sem.at[slot, d - 1],
                device_id=sector_id(d), device_id_type=MESH))
        for copy in copies:
            copy.start()
        for copy in copies:
            copy.wait()
        sums = ends[0]
        for d in range(1, n_sec):
            sums = sums + recv[slot, d - 1]
        sums = jnp.sum(sums, axis=1, keepdims=True)
        return [sums[i:i + 1, :] for i in range(len(dots))]

    def lined(slot, at, v):
        def line(d, i):
            return jnp.broadcast_to(recv[slot, d - 1, at + i:at + i + 1, :], (ROWS, LANES))
        return jnp.concatenate(
            [line(1, i) for i in range(edge)] + [v] + [line(n_sec - 1, i) for i in range(edge)], axis=1)

    def inner(x):
        return x[:, HALO:HALO + local]

    mass = spanned(0, mass_ref[...])
    states = spanned(1, st_ref[...])
    mean = tsend[...]
    for d in range(1, n_sec):
        mean = mean + trecv[d - 1]
    mean = jnp.sum(mean[0:1, :], axis=1, keepdims=True) * (1.0 / (n_sec * local))
    more = coupled([jnp.ones((ROWS, wide), jnp.float32)], 1, n_w)[0]
    sums = more[:, 2 * LANES:2 * LANES + local]
    outer = mass[:, LANES:wide - LANES] - mean + more
    core = inner(mass) - mean + sums

    def limited(step):
        return jnp.minimum(jnp.maximum(step, 1.0 / 710.0), 1.0 / 0.0029)

    def solve(rhs):
        r = rhs
        u = outer * r[:, LANES:wide - LANES] - coupled([r], 1, n_w)[0]
        u1 = u[:, 2 * LANES:2 * LANES + local]
        u2 = core * u1 - coupled([u], 2, groups)[0]
        r_in = inner(r)
        m0, m1, m2, m3 = exchange(
            0, [folded(r_in * r_in), folded(r_in * u1), folded(u1 * u1), folded(u1 * u2)],
            [(10, u1), (13, u2)])
        step = m0 / (m1 + mean * m0)
        keep = m1 / (m1 + mean * m0)
        rr = jnp.maximum(step * step * (m2 - m1 * (m1 / m0)), 1e-12 * m0)
        rb = keep * keep * m1 - 2.0 * keep * step * m2 + step * step * m3
        beta = rr / m0
        following = limited(rr / (rb + mean * rr - beta * (rr / step)))
        u1, u2 = lined(0, 10, u1), lined(0, 13, u2)
        r1 = keep * r - step * u1
        p = r1 + beta * r
        s = keep * u1 - step * u2 + beta * u1 + mean * p
        x = step * r + following * p
        r = r1 - following * s
        u = outer * r[:, LANES:wide - LANES] - coupled([r], 1, n_w)[0]
        u1 = u[:, 2 * LANES:2 * LANES + local]
        nu, ns = coupled([u, s[:, LANES:wide - LANES]], 2, groups)
        r_in, p_in, s_in = inner(r), inner(p), inner(s)
        u2, bs = core * u1 - nu, core * s_in - ns
        m0, m1, m2, m3, rs, ps, us, ss, sb, vs = exchange(
            1, [folded(a * b) for a, b in (
                (r_in, r_in), (r_in, u1), (u1, u1), (u1, u2), (r_in, s_in),
                (p_in, s_in), (u1, s_in), (s_in, s_in), (s_in, bs), (u2, s_in))],
            [(10, u1), (13, sums)])
        beta = -rs / ps
        step = limited(m0 / (m1 + mean * m0 + beta * rs))
        keep, c = 1.0 - mean * step, step * beta
        rr = (keep * keep * m0 + step * step * m2 + c * c * ss
              - 2.0 * keep * step * m1 - 2.0 * keep * c * rs + 2.0 * step * c * us)
        rr = jnp.maximum(rr, 1e-12 * m0)
        rb = (keep * keep * m1 + step * step * m3 + c * c * sb
              - 2.0 * keep * step * m2 - 2.0 * keep * c * us + 2.0 * step * c * vs)
        later = rr / m0
        following = limited(rr / (rb + mean * rr - later * (rr / step)))
        u1 = lined(1, 10, u1)
        p = r + beta * p
        s = u1 + mean * r + beta * s
        r = r - step * s
        return x + step * p + following * (r + later * p)

    def to_rows(ref, x):
        for t in range(tiles):
            ref[t:t + 1, :] = x[0:1, t * LANES:(t + 1) * LANES]

    rate = None
    for sweep in range(SWEEPS):
        def section(i, current):
            source = jnp.concatenate(
                [vrecv[0, pl.ds(2 + i, 1), :], src_ref[0, pl.ds(i, 1), :], vrecv[1, pl.ds(2 + i, 1), :]], axis=1)
            return solve(mass * current + jnp.broadcast_to(source, (ROWS, wide)))

        fine = lax.fori_loop(0, steps, section, states)
        if sweep == 0:
            rate = mass / (mass + steps * lined(1, 13, sums))
        offset = fine - rate * states
        to_rows(csend.at[sweep, 0], offset)
        to_rows(csend.at[sweep, 1], rate if sweep == 0 else fine)
        copies = [pltpu.make_async_remote_copy(
            csend.at[sweep], crecv.at[sweep, cut], cs_sem.at[sweep, d - 1], cr_sem.at[sweep, d - 1],
            device_id=cut_id(d), device_id_type=MESH) for d in range(1, n_cut)]
        for copy in copies:
            copy.start()
        crecv[sweep, cut] = csend[sweep]
        for copy in copies:
            copy.wait()
        p_run = jnp.ones((tiles, LANES), jnp.float32)
        q_run = jnp.zeros((tiles, LANES), jnp.float32)
        p_mine, q_mine = p_run, q_run
        for j in range(n_cut):
            here = cut == j
            p_mine = jnp.where(here, p_run, p_mine)
            q_mine = jnp.where(here, q_run, q_mine)
            a = crecv[0, j, 1, :tiles]
            b = crecv[sweep, j, 0, :tiles]
            p_run, q_run = a * p_run, a * q_run + b
        new = p_mine * (q_run / (1.0 - p_run)) + q_mine
        if sweep == SWEEPS - 1:
            arrived = crecv[sweep, lax.rem(cut + n_cut - 1, n_cut), 1, :tiles]
            spread[:tiles, :] = arrived
            for t in range(edge, tiles - edge):
                at = (t - edge) * LANES
                def_ref[0:1, at:at + LANES] = spread[t:t + 1, :] - states[0:1, t * LANES:(t + 1) * LANES]
                new_ref[0:1, at:at + LANES] = new[t:t + 1, :]
        else:
            spread[:tiles, :] = new
            states = jnp.concatenate(
                [jnp.broadcast_to(spread[t:t + 1, :], (ROWS, LANES)) for t in range(tiles)], axis=1)


def shards(sizes, couplings, edge_mask, slice_mass, sources, slice_states):
    n_mesh, n_sub, n_cut = sizes
    n_sec = n_mesh * n_sub
    blocks = couplings.shape[0]
    wide = blocks * BLOCK + 2 * HALO
    tiles = wide // LANES
    lines = -(-tiles // ROWS) * ROWS
    steps = sources.shape[1]
    vrows = -(-(2 + steps) // ROWS) * ROWS
    f32 = jnp.float32
    vmem = pl.BlockSpec(memory_space=pltpu.VMEM)
    out = jax.ShapeDtypeStruct(slice_states.shape, f32)
    return pl.pallas_call(
        functools.partial(kernel, sizes),
        out_shape=(out, out),
        in_specs=[pl.BlockSpec(memory_space=pl.ANY), pl.BlockSpec(memory_space=pltpu.SMEM), vmem, vmem, vmem],
        out_specs=(vmem, vmem),
        scratch_shapes=[
            pltpu.VMEM((blocks // 2 + 4, 8 * BLOCK, 2 * LANES), jnp.bfloat16),
            pltpu.VMEM((blocks + BEFORE + REACH + 1, BLOCK, 4 * BLOCK), f32),
            pltpu.VMEM((blocks + BEFORE + REACH + 1, 2, LANES), f32),
            pltpu.VMEM((2, vrows, HALO), f32),
            pltpu.VMEM((2, vrows, HALO), f32),
            pltpu.VMEM((ROWS, LANES), f32),
            pltpu.VMEM((n_sec - 1, ROWS, LANES), f32),
            pltpu.VMEM((2, 2, 2 * ROWS, LANES), f32),
            pltpu.VMEM((2, n_sec - 1, 2 * ROWS, LANES), f32),
            pltpu.VMEM((SWEEPS, 2, lines, LANES), f32),
            pltpu.VMEM((SWEEPS, n_cut, 2, lines, LANES), f32),
            pltpu.VMEM((lines, LANES), f32),
            pltpu.SemaphoreType.DMA,
            pltpu.SemaphoreType.DMA((6,)),
            pltpu.SemaphoreType.DMA((4,)),
            pltpu.SemaphoreType.DMA((4,)),
            pltpu.SemaphoreType.DMA((n_sec - 1,)),
            pltpu.SemaphoreType.DMA((n_sec - 1,)),
            pltpu.SemaphoreType.DMA((2, n_sec - 1)),
            pltpu.SemaphoreType.DMA((2, n_sec - 1)),
            pltpu.SemaphoreType.DMA((SWEEPS, n_cut - 1)),
            pltpu.SemaphoreType.DMA((SWEEPS, n_cut - 1)),
        ],
        compiler_params=pltpu.CompilerParams(
            collective_id=0, has_side_effects=True, vmem_limit_bytes=32 * 1024 * 1024),
    )(couplings, edge_mask.T, slice_mass, sources, slice_states)


def solution(mesh):
    rows = P(("groups", "cuts"), ("mesh", "sub"))
    placed = (
        P(("mesh", "sub"), None, None),
        P(("mesh", "sub"), None),
        rows,
        P(("groups", "cuts"), None, ("mesh", "sub")),
        rows,
    )
    sizes = (mesh.shape["mesh"], mesh.shape["sub"], mesh.shape["cuts"])
    return jax.shard_map(
        functools.partial(shards, sizes),
        mesh=mesh,
        in_specs=placed,
        out_specs=(rows, rows),
        check_vma=False,
    )
```

```python
import functools

import jax
import jax.numpy as jnp
from jax import lax
from jax.experimental import pallas as pl
from jax.experimental.pallas import tpu as pltpu
from jax.sharding import PartitionSpec as P

REACH = 3
CG_ITERS = 4
SWEEPS = 2
BLOCK = 64
LANES = 128
ROWS = 8
HALO = 3 * LANES
BEFORE = 2 * REACH
MESH = pl.DeviceIdType.MESH


def kernel(sizes, coup, mask, mass_in, src_in, st_in, new_out, def_out,
           mass_ref, src_ref, st_ref, new_ref, def_ref, W, ext, fac, vsend, vrecv, tsend, trecv, send, recv, csend, crecv, spread,
           isem, lsem, hsem, fsem, vsem, ts_sem, tr_sem, xs_sem, xr_sem, cs_sem, cr_sem):
    n_mesh, n_sub, n_cut = sizes
    n_sec = n_mesh * n_sub
    blocks = coup.shape[0]
    groups = blocks // 2
    local = blocks * BLOCK
    wide = local + 2 * HALO
    tiles = wide // LANES
    edge = HALO // LANES
    steps = src_in.shape[1]

    sector = lax.axis_index("mesh") * n_sub + lax.axis_index("sub")
    cut = lax.axis_index("cuts")

    def sector_id(distance):
        other = lax.rem(sector + distance, n_sec)
        return {"mesh": other // n_sub, "sub": lax.rem(other, n_sub)}

    def cut_id(distance):
        return {"cuts": lax.rem(cut + distance, n_cut)}

    barrier = pltpu.get_barrier_semaphore()
    for d in range(1, n_sec):
        pl.semaphore_signal(barrier, inc=1, device_id=sector_id(d), device_id_type=MESH)
    for d in range(1, n_cut):
        pl.semaphore_signal(barrier, inc=1, device_id=cut_id(d), device_id_type=MESH)
    fetch = pltpu.make_async_copy(coup, ext.at[BEFORE:BEFORE + blocks], lsem)
    small = [pltpu.make_async_copy(a, b, isem.at[i]) for i, (a, b) in enumerate(
        ((mass_in, mass_ref), (src_in, src_ref), (st_in, st_ref)))]
    for copy in small:
        copy.start()
    fetch.start()

    low_half = lax.broadcasted_iota(jnp.int32, (BLOCK, LANES), 1) < BLOCK
    low_row = lax.broadcasted_iota(jnp.int32, (ROWS, LANES), 1) < BLOCK
    low_line = lax.broadcasted_iota(jnp.int32, (1, LANES), 1) < BLOCK
    row = lax.broadcasted_iota(jnp.int32, (ROWS, LANES), 0)
    zero = jnp.zeros((BLOCK, LANES), jnp.float32)

    for b in range(blocks):
        m = [mask[k, b].astype(jnp.float32) for k in range(REACH)]
        fac[BEFORE + b, 0:1, :] = jnp.where(low_line, 1.0, m[0])
        fac[BEFORE + b, 1:2, :] = jnp.where(low_line, m[1], m[2])
    last = BEFORE + blocks + REACH
    fac[last] = jnp.zeros((2, LANES), jnp.float32)
    ext[last, :, :LANES] = zero
    ext[last, :, LANES:] = zero
    for b in range(2):
        ext[b, :, :LANES] = zero
    for copy in small:
        copy.wait()
    for i, at in enumerate((local - HALO, 0)):
        vsend[i, 0:1, :] = mass_ref[0:1, at:at + HALO]
        vsend[i, 1:2, :] = st_ref[0:1, at:at + HALO]
        for s in range(steps):
            vsend[i, 2 + s:3 + s, :] = src_ref[0, s:s + 1, at:at + HALO]

    def folded(x):
        parts = [x[:, i * LANES:(i + 1) * LANES] for i in range(x.shape[1] // LANES)]
        while len(parts) > 1:
            parts = [sum(parts[i:i + 2]) for i in range(0, len(parts), 2)]
        return parts[0]

    tsend[...] = jnp.broadcast_to(folded(mass_ref[...]), (ROWS, LANES))

    pl.semaphore_wait(barrier, n_sec - 1 + n_cut - 1)

    right, left = sector_id(1), sector_id(n_sec - 1)
    after = BEFORE + blocks

    def to(src, dst, sems, i, who):
        return pltpu.make_async_remote_copy(
            src, dst, sems.at[i], sems.at[i + 1], device_id=who, device_id_type=MESH)

    first = [
        to(coup.at[blocks - 4:blocks], ext.at[2:BEFORE], hsem, 0, right),
        to(coup.at[0:REACH], ext.at[after:last], hsem, 2, left),
        to(coup.at[blocks - BEFORE:blocks - 4, :, LANES:], ext.at[0:2, :, LANES:], hsem, 4, right),
        to(fac.at[blocks:after], fac.at[0:BEFORE], fsem, 0, right),
        to(fac.at[BEFORE:BEFORE + REACH], fac.at[after:last], fsem, 2, left),
        to(vsend.at[0], vrecv.at[0], vsem, 0, right),
        to(vsend.at[1], vrecv.at[1], vsem, 2, left),
    ]
    for d in range(1, n_sec):
        first.append(pltpu.make_async_remote_copy(
            tsend, trecv.at[d - 1], ts_sem.at[d - 1], tr_sem.at[d - 1],
            device_id=sector_id(d), device_id_type=MESH))
    for copy in first[3:] + first[:3]:
        copy.start()

    def turned(x):
        return pltpu.roll(x, BLOCK, 1)

    n_w = groups + 4

    def put(g, at, block):
        if not 0 <= g < n_w:
            return
        high = block.astype(jnp.bfloat16)
        low = (block - high.astype(jnp.float32)).astype(jnp.bfloat16)
        W[g, at * BLOCK:(at + 1) * BLOCK, :LANES] = high
        W[g, at * BLOCK:(at + 1) * BLOCK, LANES:] = low

    unit = lax.broadcasted_iota(jnp.int32, (BLOCK, LANES), 0) == lax.rem(
        lax.broadcasted_iota(jnp.int32, (BLOCK, LANES), 1), BLOCK)

    def masked(b):
        return ext[b, :, :LANES] * fac[b, 0:1, :], ext[b, :, LANES:] * fac[b, 1:2, :]

    def build(pair):
        g = pair + 2
        n0, f0 = masked(2 * pair + BEFORE)
        n1, f1 = masked(2 * pair + BEFORE + 1)
        n1t, f1t = turned(n1), turned(f1)
        put(g + 1, 2, f0)
        put(g + 1, 3, jnp.where(low_half, n1t, f1t))
        put(g + 2, 1, jnp.where(low_half, f1t, zero))
        if g < 0:
            return
        near_t = jnp.concatenate([n0, n1], axis=0).T
        far_t = jnp.concatenate([f0, f1], axis=0).T
        own_t, k1_t = near_t[:BLOCK], near_t[BLOCK:]
        k2_t, k3_t = far_t[:BLOCK], far_t[BLOCK:]
        put(g, 4, jnp.where(low_half, jnp.where(unit, 0.0, 0.5 * (n0 + own_t)), n0))
        put(g, 5, jnp.where(low_half, k1_t, jnp.where(unit, 0.0, 0.5 * (n1t + own_t))))
        put(g, 6, jnp.where(low_half, k2_t, k1_t))
        put(g, 7, jnp.where(low_half, k3_t, k2_t))
        put(g, 0, jnp.where(low_half, zero, k3_t))

    put(0, 1, zero)
    fetch.wait()
    for pair in range(groups):
        build(pair)
    for copy in first:
        copy.wait()
    for pair in (-3, -2, -1, groups, groups + 1):
        build(pair)

    def spanned(at, middle):
        whole = jnp.concatenate([vrecv[0, at:at + 1, :], middle, vrecv[1, at:at + 1, :]], axis=1)
        return jnp.broadcast_to(whole, (ROWS, wide))

    def total(x):
        x = x + pltpu.roll(x, 4, 0)
        x = x + pltpu.roll(x, 2, 0)
        return x + pltpu.roll(x, 1, 0)

    def tile(x, i):
        return x[:, i * LANES:(i + 1) * LANES]

    def coupled(vectors, begin, count):
        width = vectors[0].shape[1]
        rows = lax.broadcasted_iota(jnp.int32, (ROWS, width), 0)
        parts = jnp.zeros((ROWS, width), jnp.float32)
        for i, v in enumerate(vectors):
            h = v.astype(jnp.bfloat16).astype(jnp.float32)
            rest = v - h
            m = rest.astype(jnp.bfloat16).astype(jnp.float32)
            for j, part in enumerate((h, m, rest - m)):
                parts = jnp.where(rows == 3 * i + j, part, parts)
        cast = parts.astype(jnp.bfloat16)
        blank = jnp.zeros((ROWS, LANES), jnp.float32)
        n_tiles = width // LANES
        out = [[] for _ in vectors]
        for t in range(count):
            centre = t + begin
            up = tile(parts, centre + 2) if centre + 2 < n_tiles else blank
            down = tile(parts, centre - 2) if centre >= 2 else blank
            ends = jnp.where(low_row, up, down).astype(jnp.bfloat16)
            lhs = jnp.concatenate([ends, cast[:, (centre - 1) * LANES:(centre + 2) * LANES]], axis=1)
            g = t + (n_w - count) // 2
            r = jnp.dot(lhs, W[g], preferred_element_type=jnp.float32)
            r = r[:, :LANES] + r[:, LANES:]
            if len(vectors) == 1:
                out[0].append(total(r))
            else:
                out[0].append(total(jnp.where(row < 3, r, 0.0)))
                out[1].append(total(jnp.where(row < 3, 0.0, r)))
        return [jnp.concatenate(o, axis=1) for o in out]

    def stacked(values):
        halves = []
        for at in (0, ROWS):
            message = jnp.zeros((ROWS, LANES), jnp.float32)
            for i in range(ROWS):
                if at + i in values:
                    message = jnp.where(row == i, values[at + i], message)
            halves.append(message)
        return jnp.concatenate(halves, axis=0)

    def exchange(slot, dots, rims):
        ends = []
        for side in range(2):
            values = dict(enumerate(dots))
            for at, v in rims:
                for i in range(edge):
                    values[at + i] = tile(v, i if side else groups - edge + i)
            ends.append(stacked(values))
            send[slot, side] = ends[side]
        copies = []
        for d in range(1, n_sec):
            copies.append(pltpu.make_async_remote_copy(
                send.at[slot, 1 if d == n_sec - 1 else 0], recv.at[slot, d - 1],
                xs_sem.at[slot, d - 1], xr_sem.at[slot, d - 1],
                device_id=sector_id(d), device_id_type=MESH))
        for copy in copies:
            copy.start()
        for copy in copies:
            copy.wait()
        sums = ends[0]
        for d in range(1, n_sec):
            sums = sums + recv[slot, d - 1]
        sums = jnp.sum(sums, axis=1, keepdims=True)
        return [sums[i:i + 1, :] for i in range(len(dots))]

    def lined(slot, at, v):
        def line(d, i):
            return jnp.broadcast_to(recv[slot, d - 1, at + i:at + i + 1, :], (ROWS, LANES))
        return jnp.concatenate(
            [line(1, i) for i in range(edge)] + [v] + [line(n_sec - 1, i) for i in range(edge)], axis=1)

    def inner(x):
        return x[:, HALO:HALO + local]

    mass = spanned(0, mass_ref[...])
    states = spanned(1, st_ref[...])
    mean = tsend[...]
    for d in range(1, n_sec):
        mean = mean + trecv[d - 1]
    mean = jnp.sum(mean[0:1, :], axis=1, keepdims=True) * (1.0 / (n_sec * local))
    more = coupled([jnp.ones((ROWS, wide), jnp.float32)], 1, n_w)[0]
    sums = more[:, 2 * LANES:2 * LANES + local]
    outer = mass[:, LANES:wide - LANES] - mean + more
    core = inner(mass) - mean + sums

    def limited(step):
        return jnp.minimum(jnp.maximum(step, 1.0 / 710.0), 1.0 / 0.0029)

    def solve(rhs):
        r = rhs
        u = outer * r[:, LANES:wide - LANES] - coupled([r], 1, n_w)[0]
        u1 = u[:, 2 * LANES:2 * LANES + local]
        u2 = core * u1 - coupled([u], 2, groups)[0]
        r_in = inner(r)
        m0, m1, m2, m3 = exchange(
            0, [folded(r_in * r_in), folded(r_in * u1), folded(u1 * u1), folded(u1 * u2)],
            [(10, u1), (13, u2)])
        step = m0 / (m1 + mean * m0)
        keep = m1 / (m1 + mean * m0)
        rr = jnp.maximum(step * step * (m2 - m1 * (m1 / m0)), 1e-12 * m0)
        rb = keep * keep * m1 - 2.0 * keep * step * m2 + step * step * m3
        beta = rr / m0
        following = limited(rr / (rb + mean * rr - beta * (rr / step)))
        u1, u2 = lined(0, 10, u1), lined(0, 13, u2)
        r1 = keep * r - step * u1
        p = r1 + beta * r
        s = keep * u1 - step * u2 + beta * u1 + mean * p
        x = step * r + following * p
        r = r1 - following * s
        u = outer * r[:, LANES:wide - LANES] - coupled([r], 1, n_w)[0]
        u1 = u[:, 2 * LANES:2 * LANES + local]
        nu, ns = coupled([u, s[:, LANES:wide - LANES]], 2, groups)
        r_in, p_in, s_in = inner(r), inner(p), inner(s)
        u2, bs = core * u1 - nu, core * s_in - ns
        m0, m1, m2, m3, rs, ps, us, ss, sb, vs = exchange(
            1, [folded(a * b) for a, b in (
                (r_in, r_in), (r_in, u1), (u1, u1), (u1, u2), (r_in, s_in),
                (p_in, s_in), (u1, s_in), (s_in, s_in), (s_in, bs), (u2, s_in))],
            [(10, u1), (13, sums)])
        beta = -rs / ps
        step = limited(m0 / (m1 + mean * m0 + beta * rs))
        keep, c = 1.0 - mean * step, step * beta
        rr = (keep * keep * m0 + step * step * m2 + c * c * ss
              - 2.0 * keep * step * m1 - 2.0 * keep * c * rs + 2.0 * step * c * us)
        rr = jnp.maximum(rr, 1e-12 * m0)
        rb = (keep * keep * m1 + step * step * m3 + c * c * sb
              - 2.0 * keep * step * m2 - 2.0 * keep * c * us + 2.0 * step * c * vs)
        later = rr / m0
        following = limited(rr / (rb + mean * rr - later * (rr / step)))
        u1 = lined(1, 10, u1)
        p = r + beta * p
        s = u1 + mean * r + beta * s
        r = r - step * s
        return x + step * p + following * (r + later * p)

    def to_rows(ref, x):
        for t in range(tiles):
            ref[t:t + 1, :] = x[0:1, t * LANES:(t + 1) * LANES]

    rate = None
    for sweep in range(SWEEPS):
        def section(i, current):
            source = jnp.concatenate(
                [vrecv[0, pl.ds(2 + i, 1), :], src_ref[0, pl.ds(i, 1), :], vrecv[1, pl.ds(2 + i, 1), :]], axis=1)
            return solve(mass * current + jnp.broadcast_to(source, (ROWS, wide)))

        fine = lax.fori_loop(0, steps, section, states)
        if sweep == 0:
            rate = mass / (mass + steps * lined(1, 13, sums))
        offset = fine - rate * states
        to_rows(csend.at[sweep, 0], offset)
        to_rows(csend.at[sweep, 1], rate if sweep == 0 else fine)
        copies = [pltpu.make_async_remote_copy(
            csend.at[sweep], crecv.at[sweep, cut], cs_sem.at[sweep, d - 1], cr_sem.at[sweep, d - 1],
            device_id=cut_id(d), device_id_type=MESH) for d in range(1, n_cut)]
        for copy in copies:
            copy.start()
        crecv[sweep, cut] = csend[sweep]
        for copy in copies:
            copy.wait()
        p_run = jnp.ones((tiles, LANES), jnp.float32)
        q_run = jnp.zeros((tiles, LANES), jnp.float32)
        p_mine, q_mine = p_run, q_run
        for j in range(n_cut):
            here = cut == j
            p_mine = jnp.where(here, p_run, p_mine)
            q_mine = jnp.where(here, q_run, q_mine)
            a = crecv[0, j, 1, :tiles]
            b = crecv[sweep, j, 0, :tiles]
            p_run, q_run = a * p_run, a * q_run + b
        new = p_mine * (q_run / (1.0 - p_run)) + q_mine
        if sweep == SWEEPS - 1:
            arrived = crecv[sweep, lax.rem(cut + n_cut - 1, n_cut), 1, :tiles]
            spread[:tiles, :] = arrived
            for t in range(edge, tiles - edge):
                at = (t - edge) * LANES
                def_ref[0:1, at:at + LANES] = spread[t:t + 1, :] - states[0:1, t * LANES:(t + 1) * LANES]
                new_ref[0:1, at:at + LANES] = new[t:t + 1, :]
            ends = [pltpu.make_async_copy(a, b, isem.at[3 + i]) for i, (a, b) in enumerate(
                ((new_ref, new_out), (def_ref, def_out)))]
            for copy in ends:
                copy.start()
            for copy in ends:
                copy.wait()
        else:
            spread[:tiles, :] = new
            states = jnp.concatenate(
                [jnp.broadcast_to(spread[t:t + 1, :], (ROWS, LANES)) for t in range(tiles)], axis=1)


def shards(sizes, couplings, edge_mask, slice_mass, sources, slice_states):
    n_mesh, n_sub, n_cut = sizes
    n_sec = n_mesh * n_sub
    blocks = couplings.shape[0]
    wide = blocks * BLOCK + 2 * HALO
    tiles = wide // LANES
    lines = -(-tiles // ROWS) * ROWS
    steps = sources.shape[1]
    vrows = -(-(2 + steps) // ROWS) * ROWS
    f32 = jnp.float32
    hbm = pl.BlockSpec(memory_space=pltpu.HBM)
    out = jax.ShapeDtypeStruct(slice_states.shape, f32)
    return pl.pallas_call(
        functools.partial(kernel, sizes),
        out_shape=(out, out),
        in_specs=[hbm, pl.BlockSpec(memory_space=pltpu.SMEM), hbm, hbm, hbm],
        out_specs=(hbm, hbm),
        scratch_shapes=[
            pltpu.VMEM(slice_mass.shape, f32),
            pltpu.VMEM(sources.shape, f32),
            pltpu.VMEM(slice_states.shape, f32),
            pltpu.VMEM(slice_states.shape, f32),
            pltpu.VMEM(slice_states.shape, f32),
            pltpu.VMEM((blocks // 2 + 4, 8 * BLOCK, 2 * LANES), jnp.bfloat16),
            pltpu.VMEM((blocks + BEFORE + REACH + 1, BLOCK, 4 * BLOCK), f32),
            pltpu.VMEM((blocks + BEFORE + REACH + 1, 2, LANES), f32),
            pltpu.VMEM((2, vrows, HALO), f32),
            pltpu.VMEM((2, vrows, HALO), f32),
            pltpu.VMEM((ROWS, LANES), f32),
            pltpu.VMEM((n_sec - 1, ROWS, LANES), f32),
            pltpu.VMEM((2, 2, 2 * ROWS, LANES), f32),
            pltpu.VMEM((2, n_sec - 1, 2 * ROWS, LANES), f32),
            pltpu.VMEM((SWEEPS, 2, lines, LANES), f32),
            pltpu.VMEM((SWEEPS, n_cut, 2, lines, LANES), f32),
            pltpu.VMEM((lines, LANES), f32),
            pltpu.SemaphoreType.DMA((5,)),
            pltpu.SemaphoreType.DMA,
            pltpu.SemaphoreType.DMA((6,)),
            pltpu.SemaphoreType.DMA((4,)),
            pltpu.SemaphoreType.DMA((4,)),
            pltpu.SemaphoreType.DMA((n_sec - 1,)),
            pltpu.SemaphoreType.DMA((n_sec - 1,)),
            pltpu.SemaphoreType.DMA((2, n_sec - 1)),
            pltpu.SemaphoreType.DMA((2, n_sec - 1)),
            pltpu.SemaphoreType.DMA((SWEEPS, n_cut - 1)),
            pltpu.SemaphoreType.DMA((SWEEPS, n_cut - 1)),
        ],
        compiler_params=pltpu.CompilerParams(
            collective_id=0, has_side_effects=True, vmem_limit_bytes=62 * 1024 * 1024),
    )(couplings, edge_mask.T, slice_mass, sources, slice_states)


def solution(mesh):
    rows = P(("groups", "cuts"), ("mesh", "sub"))
    placed = (
        P(("mesh", "sub"), None, None),
        P(("mesh", "sub"), None),
        rows,
        P(("groups", "cuts"), None, ("mesh", "sub")),
        rows,
    )
    sizes = (mesh.shape["mesh"], mesh.shape["sub"], mesh.shape["cuts"])
    return jax.shard_map(
        functools.partial(shards, sizes),
        mesh=mesh,
        in_specs=placed,
        out_specs=(rows, rows),
        check_vma=False,
    )
```

```python
import functools

import jax
import jax.numpy as jnp
from jax import lax
from jax.experimental import pallas as pl
from jax.experimental.pallas import tpu as pltpu
from jax.sharding import PartitionSpec as P

REACH = 3
CG_ITERS = 4
SWEEPS = 2
BLOCK = 64
LANES = 128
ROWS = 8
HALO = 3 * LANES
BEFORE = 2 * REACH
MESH = pl.DeviceIdType.MESH


def kernel(sizes, coup, mask, mass_in, src_in, st_in, both_ref,
           mass_ref, src_ref, st_ref, W, ext, fac, vsend, vrecv, tsend, trecv, send, recv, csend, crecv, spread,
           isem, lsem, hsem, fsem, vsem, ts_sem, tr_sem, xs_sem, xr_sem, cs_sem, cr_sem):
    n_mesh, n_sub, n_cut = sizes
    n_sec = n_mesh * n_sub
    blocks = coup.shape[0]
    groups = blocks // 2
    local = blocks * BLOCK
    wide = local + 2 * HALO
    tiles = wide // LANES
    edge = HALO // LANES
    steps = src_in.shape[1]
    new_ref, def_ref = both_ref.at[0], both_ref.at[1]

    sector = lax.axis_index("mesh") * n_sub + lax.axis_index("sub")
    cut = lax.axis_index("cuts")

    def sector_id(distance):
        other = lax.rem(sector + distance, n_sec)
        return {"mesh": other // n_sub, "sub": lax.rem(other, n_sub)}

    def cut_id(distance):
        return {"cuts": lax.rem(cut + distance, n_cut)}

    barrier = pltpu.get_barrier_semaphore()
    for d in range(1, n_sec):
        pl.semaphore_signal(barrier, inc=1, device_id=sector_id(d), device_id_type=MESH)
    for d in range(1, n_cut):
        pl.semaphore_signal(barrier, inc=1, device_id=cut_id(d), device_id_type=MESH)
    fetch = pltpu.make_async_copy(coup, ext.at[BEFORE:BEFORE + blocks], lsem)
    small = [pltpu.make_async_copy(a, b, isem.at[i]) for i, (a, b) in enumerate(
        ((mass_in, mass_ref), (src_in, src_ref), (st_in, st_ref)))]
    for copy in small:
        copy.start()
    fetch.start()

    low_half = lax.broadcasted_iota(jnp.int32, (BLOCK, LANES), 1) < BLOCK
    low_row = lax.broadcasted_iota(jnp.int32, (ROWS, LANES), 1) < BLOCK
    low_line = lax.broadcasted_iota(jnp.int32, (1, LANES), 1) < BLOCK
    row = lax.broadcasted_iota(jnp.int32, (ROWS, LANES), 0)
    zero = jnp.zeros((BLOCK, LANES), jnp.float32)

    for b in range(blocks):
        m = [mask[k, b].astype(jnp.float32) for k in range(REACH)]
        fac[BEFORE + b, 0:1, :] = jnp.where(low_line, 1.0, m[0])
        fac[BEFORE + b, 1:2, :] = jnp.where(low_line, m[1], m[2])
    last = BEFORE + blocks + REACH
    fac[last] = jnp.zeros((2, LANES), jnp.float32)
    ext[last, :, :LANES] = zero
    ext[last, :, LANES:] = zero
    for b in range(2):
        ext[b, :, :LANES] = zero
    for copy in small:
        copy.wait()
    for i, at in enumerate((local - HALO, 0)):
        vsend[i, 0:1, :] = mass_ref[0:1, at:at + HALO]
        vsend[i, 1:2, :] = st_ref[0:1, at:at + HALO]
        for s in range(steps):
            vsend[i, 2 + s:3 + s, :] = src_ref[0, s:s + 1, at:at + HALO]

    def folded(x):
        parts = [x[:, i * LANES:(i + 1) * LANES] for i in range(x.shape[1] // LANES)]
        while len(parts) > 1:
            parts = [sum(parts[i:i + 2]) for i in range(0, len(parts), 2)]
        return parts[0]

    tsend[...] = jnp.broadcast_to(folded(mass_ref[...]), (ROWS, LANES))

    pl.semaphore_wait(barrier, n_sec - 1 + n_cut - 1)

    right, left = sector_id(1), sector_id(n_sec - 1)
    after = BEFORE + blocks

    def to(src, dst, sems, i, who):
        return pltpu.make_async_remote_copy(
            src, dst, sems.at[i], sems.at[i + 1], device_id=who, device_id_type=MESH)

    first = [
        to(coup.at[blocks - 4:blocks], ext.at[2:BEFORE], hsem, 0, right),
        to(coup.at[0:REACH], ext.at[after:last], hsem, 2, left),
        to(coup.at[blocks - BEFORE:blocks - 4, :, LANES:], ext.at[0:2, :, LANES:], hsem, 4, right),
        to(fac.at[blocks:after], fac.at[0:BEFORE], fsem, 0, right),
        to(fac.at[BEFORE:BEFORE + REACH], fac.at[after:last], fsem, 2, left),
        to(vsend.at[0], vrecv.at[0], vsem, 0, right),
        to(vsend.at[1], vrecv.at[1], vsem, 2, left),
    ]
    for d in range(1, n_sec):
        first.append(pltpu.make_async_remote_copy(
            tsend, trecv.at[d - 1], ts_sem.at[d - 1], tr_sem.at[d - 1],
            device_id=sector_id(d), device_id_type=MESH))
    for copy in first:
        copy.start()

    def turned(x):
        return pltpu.roll(x, BLOCK, 1)

    n_w = groups + 4

    def put(g, at, block):
        if not 0 <= g < n_w:
            return
        high = block.astype(jnp.bfloat16)
        low = (block - high.astype(jnp.float32)).astype(jnp.bfloat16)
        W[g, at * BLOCK:(at + 1) * BLOCK, :LANES] = high
        W[g, at * BLOCK:(at + 1) * BLOCK, LANES:] = low

    unit = lax.broadcasted_iota(jnp.int32, (BLOCK, LANES), 0) == lax.rem(
        lax.broadcasted_iota(jnp.int32, (BLOCK, LANES), 1), BLOCK)

    def masked(b):
        return ext[b, :, :LANES] * fac[b, 0:1, :], ext[b, :, LANES:] * fac[b, 1:2, :]

    def build(pair):
        g = pair + 2
        n0, f0 = masked(2 * pair + BEFORE)
        n1, f1 = masked(2 * pair + BEFORE + 1)
        n1t, f1t = turned(n1), turned(f1)
        put(g + 1, 2, f0)
        put(g + 1, 3, jnp.where(low_half, n1t, f1t))
        put(g + 2, 1, jnp.where(low_half, f1t, zero))
        if g < 0:
            return
        near_t = jnp.concatenate([n0, n1], axis=0).T
        far_t = jnp.concatenate([f0, f1], axis=0).T
        own_t, k1_t = near_t[:BLOCK], near_t[BLOCK:]
        k2_t, k3_t = far_t[:BLOCK], far_t[BLOCK:]
        put(g, 4, jnp.where(low_half, jnp.where(unit, 0.0, 0.5 * (n0 + own_t)), n0))
        put(g, 5, jnp.where(low_half, k1_t, jnp.where(unit, 0.0, 0.5 * (n1t + own_t))))
        put(g, 6, jnp.where(low_half, k2_t, k1_t))
        put(g, 7, jnp.where(low_half, k3_t, k2_t))
        put(g, 0, jnp.where(low_half, zero, k3_t))

    put(0, 1, zero)
    fetch.wait()
    for pair in range(groups):
        build(pair)
    for copy in first:
        copy.wait()
    for pair in (-3, -2, -1, groups, groups + 1):
        build(pair)

    def spanned(at, middle):
        whole = jnp.concatenate([vrecv[0, at:at + 1, :], middle, vrecv[1, at:at + 1, :]], axis=1)
        return jnp.broadcast_to(whole, (ROWS, wide))

    def total(x):
        x = x + pltpu.roll(x, 4, 0)
        x = x + pltpu.roll(x, 2, 0)
        return x + pltpu.roll(x, 1, 0)

    def tile(x, i):
        return x[:, i * LANES:(i + 1) * LANES]

    def coupled(vectors, begin, count):
        width = vectors[0].shape[1]
        rows = lax.broadcasted_iota(jnp.int32, (ROWS, width), 0)
        parts = jnp.zeros((ROWS, width), jnp.float32)
        for i, v in enumerate(vectors):
            h = v.astype(jnp.bfloat16).astype(jnp.float32)
            rest = v - h
            m = rest.astype(jnp.bfloat16).astype(jnp.float32)
            for j, part in enumerate((h, m, rest - m)):
                parts = jnp.where(rows == 3 * i + j, part, parts)
        cast = parts.astype(jnp.bfloat16)
        blank = jnp.zeros((ROWS, LANES), jnp.float32)
        n_tiles = width // LANES
        out = [[] for _ in vectors]
        for t in range(count):
            centre = t + begin
            up = tile(parts, centre + 2) if centre + 2 < n_tiles else blank
            down = tile(parts, centre - 2) if centre >= 2 else blank
            ends = jnp.where(low_row, up, down).astype(jnp.bfloat16)
            lhs = jnp.concatenate([ends, cast[:, (centre - 1) * LANES:(centre + 2) * LANES]], axis=1)
            g = t + (n_w - count) // 2
            r = jnp.dot(lhs, W[g], preferred_element_type=jnp.float32)
            r = r[:, :LANES] + r[:, LANES:]
            if len(vectors) == 1:
                out[0].append(total(r))
            else:
                out[0].append(total(jnp.where(row < 3, r, 0.0)))
                out[1].append(total(jnp.where(row < 3, 0.0, r)))
        return [jnp.concatenate(o, axis=1) for o in out]

    def stacked(values):
        halves = []
        for at in (0, ROWS):
            message = jnp.zeros((ROWS, LANES), jnp.float32)
            for i in range(ROWS):
                if at + i in values:
                    message = jnp.where(row == i, values[at + i], message)
            halves.append(message)
        return jnp.concatenate(halves, axis=0)

    def exchange(slot, dots, rims):
        ends = []
        for side in range(2):
            values = dict(enumerate(dots))
            for at, v in rims:
                for i in range(edge):
                    values[at + i] = tile(v, i if side else groups - edge + i)
            ends.append(stacked(values))
            send[slot, side] = ends[side]
        copies = []
        for d in range(1, n_sec):
            copies.append(pltpu.make_async_remote_copy(
                send.at[slot, 1 if d == n_sec - 1 else 0], recv.at[slot, d - 1],
                xs_sem.at[slot, d - 1], xr_sem.at[slot, d - 1],
                device_id=sector_id(d), device_id_type=MESH))
        for copy in copies:
            copy.start()
        for copy in copies:
            copy.wait()
        sums = ends[0]
        for d in range(1, n_sec):
            sums = sums + recv[slot, d - 1]
        sums = jnp.sum(sums, axis=1, keepdims=True)
        return [sums[i:i + 1, :] for i in range(len(dots))]

    def lined(slot, at, v):
        def line(d, i):
            return jnp.broadcast_to(recv[slot, d - 1, at + i:at + i + 1, :], (ROWS, LANES))
        return jnp.concatenate(
            [line(1, i) for i in range(edge)] + [v] + [line(n_sec - 1, i) for i in range(edge)], axis=1)

    def inner(x):
        return x[:, HALO:HALO + local]

    mass = spanned(0, mass_ref[...])
    states = spanned(1, st_ref[...])
    mean = tsend[...]
    for d in range(1, n_sec):
        mean = mean + trecv[d - 1]
    mean = jnp.sum(mean[0:1, :], axis=1, keepdims=True) * (1.0 / (n_sec * local))
    more = coupled([jnp.ones((ROWS, wide), jnp.float32)], 1, n_w)[0]
    sums = more[:, 2 * LANES:2 * LANES + local]
    outer = mass[:, LANES:wide - LANES] - mean + more
    core = inner(mass) - mean + sums

    def limited(step):
        return jnp.minimum(jnp.maximum(step, 1.0 / 710.0), 1.0 / 0.0029)

    def solve(rhs):
        r = rhs
        u = outer * r[:, LANES:wide - LANES] - coupled([r], 1, n_w)[0]
        u1 = u[:, 2 * LANES:2 * LANES + local]
        u2 = core * u1 - coupled([u], 2, groups)[0]
        r_in = inner(r)
        m0, m1, m2, m3 = exchange(
            0, [folded(r_in * r_in), folded(r_in * u1), folded(u1 * u1), folded(u1 * u2)],
            [(10, u1), (13, u2)])
        step = m0 / (m1 + mean * m0)
        keep = m1 / (m1 + mean * m0)
        rr = jnp.maximum(step * step * (m2 - m1 * (m1 / m0)), 1e-12 * m0)
        rb = keep * keep * m1 - 2.0 * keep * step * m2 + step * step * m3
        beta = rr / m0
        following = limited(rr / (rb + mean * rr - beta * (rr / step)))
        u1, u2 = lined(0, 10, u1), lined(0, 13, u2)
        r1 = keep * r - step * u1
        p = r1 + beta * r
        s = keep * u1 - step * u2 + beta * u1 + mean * p
        x = step * r + following * p
        r = r1 - following * s
        u = outer * r[:, LANES:wide - LANES] - coupled([r], 1, n_w)[0]
        u1 = u[:, 2 * LANES:2 * LANES + local]
        nu, ns = coupled([u, s[:, LANES:wide - LANES]], 2, groups)
        r_in, p_in, s_in = inner(r), inner(p), inner(s)
        u2, bs = core * u1 - nu, core * s_in - ns
        m0, m1, m2, m3, rs, ps, us, ss, sb, vs = exchange(
            1, [folded(a * b) for a, b in (
                (r_in, r_in), (r_in, u1), (u1, u1), (u1, u2), (r_in, s_in),
                (p_in, s_in), (u1, s_in), (s_in, s_in), (s_in, bs), (u2, s_in))],
            [(10, u1), (13, sums)])
        beta = -rs / ps
        step = limited(m0 / (m1 + mean * m0 + beta * rs))
        keep, c = 1.0 - mean * step, step * beta
        rr = (keep * keep * m0 + step * step * m2 + c * c * ss
              - 2.0 * keep * step * m1 - 2.0 * keep * c * rs + 2.0 * step * c * us)
        rr = jnp.maximum(rr, 1e-12 * m0)
        rb = (keep * keep * m1 + step * step * m3 + c * c * sb
              - 2.0 * keep * step * m2 - 2.0 * keep * c * us + 2.0 * step * c * vs)
        later = rr / m0
        following = limited(rr / (rb + mean * rr - later * (rr / step)))
        u1 = lined(1, 10, u1)
        p = r + beta * p
        s = u1 + mean * r + beta * s
        r = r - step * s
        return x + step * p + following * (r + later * p)

    def to_rows(ref, x):
        for t in range(tiles):
            ref[t:t + 1, :] = x[0:1, t * LANES:(t + 1) * LANES]

    rate = None
    for sweep in range(SWEEPS):
        def section(i, current):
            source = jnp.concatenate(
                [vrecv[0, pl.ds(2 + i, 1), :], src_ref[0, pl.ds(i, 1), :], vrecv[1, pl.ds(2 + i, 1), :]], axis=1)
            return solve(mass * current + jnp.broadcast_to(source, (ROWS, wide)))

        fine = lax.fori_loop(0, steps, section, states)
        if sweep == 0:
            rate = mass / (mass + steps * lined(1, 13, sums))
        offset = fine - rate * states
        to_rows(csend.at[sweep, 0], offset)
        to_rows(csend.at[sweep, 1], rate if sweep == 0 else fine)
        copies = [pltpu.make_async_remote_copy(
            csend.at[sweep], crecv.at[sweep, cut], cs_sem.at[sweep, d - 1], cr_sem.at[sweep, d - 1],
            device_id=cut_id(d), device_id_type=MESH) for d in range(1, n_cut)]
        for copy in copies:
            copy.start()
        crecv[sweep, cut] = csend[sweep]
        for copy in copies:
            copy.wait()
        p_run = jnp.ones((tiles, LANES), jnp.float32)
        q_run = jnp.zeros((tiles, LANES), jnp.float32)
        p_mine, q_mine = p_run, q_run
        for j in range(n_cut):
            here = cut == j
            p_mine = jnp.where(here, p_run, p_mine)
            q_mine = jnp.where(here, q_run, q_mine)
            a = crecv[0, j, 1, :tiles]
            b = crecv[sweep, j, 0, :tiles]
            p_run, q_run = a * p_run, a * q_run + b
        new = p_mine * (q_run / (1.0 - p_run)) + q_mine
        if sweep == SWEEPS - 1:
            arrived = crecv[sweep, lax.rem(cut + n_cut - 1, n_cut), 1, :tiles]
            spread[:tiles, :] = arrived
            for t in range(edge, tiles - edge):
                at = (t - edge) * LANES
                def_ref[0:1, at:at + LANES] = spread[t:t + 1, :] - states[0:1, t * LANES:(t + 1) * LANES]
                new_ref[0:1, at:at + LANES] = new[t:t + 1, :]
        else:
            spread[:tiles, :] = new
            states = jnp.concatenate(
                [jnp.broadcast_to(spread[t:t + 1, :], (ROWS, LANES)) for t in range(tiles)], axis=1)


def shards(sizes, couplings, edge_mask, slice_mass, sources, slice_states):
    n_mesh, n_sub, n_cut = sizes
    n_sec = n_mesh * n_sub
    blocks = couplings.shape[0]
    wide = blocks * BLOCK + 2 * HALO
    tiles = wide // LANES
    lines = -(-tiles // ROWS) * ROWS
    steps = sources.shape[1]
    vrows = -(-(2 + steps) // ROWS) * ROWS
    f32 = jnp.float32
    vmem = pl.BlockSpec(memory_space=pltpu.VMEM)
    hbm = pl.BlockSpec(memory_space=pltpu.HBM)
    out = jax.ShapeDtypeStruct((2,) + slice_states.shape, f32)
    both = pl.pallas_call(
        functools.partial(kernel, sizes),
        out_shape=out,
        in_specs=[hbm, pl.BlockSpec(memory_space=pltpu.SMEM), hbm, hbm, hbm],
        out_specs=vmem,
        scratch_shapes=[
            pltpu.VMEM(slice_mass.shape, f32),
            pltpu.VMEM(sources.shape, f32),
            pltpu.VMEM(slice_states.shape, f32),
            pltpu.VMEM((blocks // 2 + 4, 8 * BLOCK, 2 * LANES), jnp.bfloat16),
            pltpu.VMEM((blocks + BEFORE + REACH + 1, BLOCK, 4 * BLOCK), f32),
            pltpu.VMEM((blocks + BEFORE + REACH + 1, 2, LANES), f32),
            pltpu.VMEM((2, vrows, HALO), f32),
            pltpu.VMEM((2, vrows, HALO), f32),
            pltpu.VMEM((ROWS, LANES), f32),
            pltpu.VMEM((n_sec - 1, ROWS, LANES), f32),
            pltpu.VMEM((2, 2, 2 * ROWS, LANES), f32),
            pltpu.VMEM((2, n_sec - 1, 2 * ROWS, LANES), f32),
            pltpu.VMEM((SWEEPS, 2, lines, LANES), f32),
            pltpu.VMEM((SWEEPS, n_cut, 2, lines, LANES), f32),
            pltpu.VMEM((lines, LANES), f32),
            pltpu.SemaphoreType.DMA((3,)),
            pltpu.SemaphoreType.DMA,
            pltpu.SemaphoreType.DMA((6,)),
            pltpu.SemaphoreType.DMA((4,)),
            pltpu.SemaphoreType.DMA((4,)),
            pltpu.SemaphoreType.DMA((n_sec - 1,)),
            pltpu.SemaphoreType.DMA((n_sec - 1,)),
            pltpu.SemaphoreType.DMA((2, n_sec - 1)),
            pltpu.SemaphoreType.DMA((2, n_sec - 1)),
            pltpu.SemaphoreType.DMA((SWEEPS, n_cut - 1)),
            pltpu.SemaphoreType.DMA((SWEEPS, n_cut - 1)),
        ],
        compiler_params=pltpu.CompilerParams(
            collective_id=0, has_side_effects=True, vmem_limit_bytes=62 * 1024 * 1024),
    )(couplings, edge_mask.T, slice_mass, sources, slice_states)
    return both[0], both[1]


def solution(mesh):
    rows = P(("groups", "cuts"), ("mesh", "sub"))
    placed = (
        P(("mesh", "sub"), None, None),
        P(("mesh", "sub"), None),
        rows,
        P(("groups", "cuts"), None, ("mesh", "sub")),
        rows,
    )
    sizes = (mesh.shape["mesh"], mesh.shape["sub"], mesh.shape["cuts"])
    return jax.shard_map(
        functools.partial(shards, sizes),
        mesh=mesh,
        in_specs=placed,
        out_specs=(rows, rows),
        check_vma=False,
    )
```
